128 devices in a mesh: dp: 4 (over z_hi, core), space: 32 (over x, y, z_lo).
Axes of the slice: x: 4, y: 4, z: 4 (z_hi: 2, z_lo: 2; z = z_hi * 2 + z_lo), core: 2. Of those that a mesh axis runs over, the one named last changes fastest.
Arguments:
- features: bfloat16 [4, 128, 64, 64, 256], P('dp', 'space'), may hold values from -6 to 6
- out_grad: bfloat16 [4, 128, 32, 32, 512], P('dp', 'space'), may hold values from -6 to 6
- reduce_weight: bfloat16 [256, 128], replicated, may hold values from -0.375 to 0.375
- spatial_weight: bfloat16 [1152, 128], replicated, may hold values from -0.1875 to 0.1875
- expand_weight: bfloat16 [128, 512], replicated, may hold values from -0.5 to 0.5
- project_weight: bfloat16 [256, 512], replicated, may hold values from -0.375 to 0.375
- reduce_bias: float32 [128], replicated, may hold values from -3 to 3
- spatial_bias: float32 [128], replicated, may hold values from -3 to 3
- output_bias: float32 [512], replicated, may hold values from -3 to 3
- live_count: int32 [4, 32], P('dp', 'space'), may hold values from 1 to 4, as said below
- neighbours: int32 [4, 128, 8], P('dp', 'space'), may hold values from -1 to 127, as said below
Outputs:
- feature_grad: bfloat16 [4, 128, 64, 64, 256], P('dp', 'space')
- reduce_grad: float32 [256, 128], replicated
- spatial_grad: float32 [1152, 128], replicated
- expand_grad: float32 [128, 512], replicated
- project_grad: float32 [256, 512], replicated
The draws below stay inside these ranges and needn't reach their ends.
Inputs may be any that keep to these rules, and one draw needn't show every extreme that they name: The first live_count slots of a device hold tissue tiles, the others are empty; in every slide some device has all 4 slots live. `neighbours`: directions 0 to 7 are up-left, up, up-right, left, right, down-left, down, down-right on the slide's grid of 16 x 8 tiles; an entry names the slot, in the same slide, of the live tile in that direction, or -1 where that grid cell is outside the grid or not live; empty slots have -1 everywhere; if slot a names b in one direction, b names a in the opposite one.
All inputs are finite; a program needn't handle non-finite values.
Results may differ from the reference program's by a relative error of at most 0.0062.
Values may be sent and summed in bfloat16 or wider, within the bound.
A program may use at most 192 MiB of HBM per device.

```python
import math
import jax
import jax.numpy as jnp
from jax import lax

CIN = 256
CM = 128
COUT = 512
S = 32
TILES_DEV = 4
GRID_C = 8
SLIDES = 4
TILES = 128
GRID_R = 16


def tissue_layout(key):
    key = jax.random.fold_in(key, 11)
    key_small, key_full, key_pick, key_cells = jax.random.split(key, 4)
    groups = TILES // TILES_DEV
    small = jax.random.randint(key_small, (SLIDES, groups), 1, max(TILES_DEV // 2, 1) + 1)
    full = jax.random.randint(key_full, (SLIDES, groups), 0, 4) == 0
    chosen = jax.random.randint(key_pick, (SLIDES,), 0, groups)
    full = full | (jnp.arange(groups, dtype=jnp.int32)[None, :] == chosen[:, None])
    counts = jnp.where(full, TILES_DEV, small).astype(jnp.int32)
    slide_keys = jax.random.split(key_cells, SLIDES)
    cells = jax.vmap(lambda one_key: jax.random.permutation(one_key, TILES))(slide_keys).astype(jnp.int32)
    slot_at = jnp.argsort(cells, axis=1).astype(jnp.int32)
    slot_ids = jnp.arange(TILES, dtype=jnp.int32)
    live = slot_ids[None, :] % TILES_DEV < jnp.repeat(counts, TILES_DEV, axis=1)
    grid_row = cells // GRID_C
    grid_col = cells % GRID_C
    columns = []
    for step_row, step_col in ((-1, -1), (-1, 0), (-1, 1), (0, -1), (0, 1), (1, -1), (1, 0), (1, 1)):
        new_row = grid_row + step_row
        new_col = grid_col + step_col
        inside = (new_row >= 0) & (new_row < GRID_R) & (new_col >= 0) & (new_col < GRID_C)
        target_cell = jnp.clip(new_row, 0, GRID_R - 1) * GRID_C + jnp.clip(new_col, 0, GRID_C - 1)
        other = jnp.take_along_axis(slot_at, target_cell, axis=1)
        other_live = jnp.take_along_axis(live, other, axis=1)
        valid = inside & live & other_live
        columns.append(jnp.where(valid, other, -1))
    links = jnp.stack(columns, -1).astype(jnp.int32)
    return (counts, links)


def draw_live_count(key, part):
    return tissue_layout(key)[0]


def draw_neighbours(key, part):
    return tissue_layout(key)[1]


def levels(key, extent, pieces, low, high):
    level, own = 1.0, jax.random.fold_in(key, 6)
    for axis_at, blocks in pieces:
        heights = jnp.exp(jax.random.uniform(jax.random.fold_in(own, axis_at), (blocks,), jnp.float32, low / len(pieces), high / len(pieces)))
        level = level * jnp.repeat(heights, extent[axis_at] // blocks).reshape([-1 if axis == axis_at else 1 for axis in range(len(extent))])
    return level


def normal_values(stream_key, extent, width, reach, pieces=(), kind=jnp.bfloat16):
    values = jax.random.normal(stream_key, extent, jnp.float32) * width
    if len(pieces) > 0:
        values = levels(stream_key, extent, pieces, -0.22, 0.18) * values
    return jnp.clip(values, min=-reach, max=reach).astype(kind)


def setup_inputs(seed: int = 0) -> dict:
    key_of = jax.random.split(jax.random.key(seed), 12)
    features = normal_values(key_of[0], (SLIDES, TILES, 2 * S, 2 * S, CIN), 1.0, 6.0, ((0, 4), (1, 32)))
    out_grad = normal_values(key_of[1], (SLIDES, TILES, S, S, COUT), 1.0, 6.0, ((0, 4), (1, 32)))
    reduce_weight = normal_values(key_of[2], (CIN, CM), CIN ** -0.5, 0.375)
    spatial_weight = normal_values(key_of[3], (9 * CM, CM), (9 * CM) ** -0.5, 0.1875)
    expand_weight = normal_values(key_of[4], (CM, COUT), CM ** -0.5, 0.5)
    project_weight = normal_values(key_of[5], (CIN, COUT), CIN ** -0.5, 0.375)
    reduce_bias = normal_values(key_of[6], (CM,), 0.5, 3.0, (), jnp.float32)
    spatial_bias = normal_values(key_of[7], (CM,), 0.5, 3.0, (), jnp.float32)
    output_bias = normal_values(key_of[8], (COUT,), 0.5, 3.0, (), jnp.float32)
    live_count = draw_live_count(jax.random.fold_in(key_of[11], 71), 0)
    neighbours = draw_neighbours(jax.random.fold_in(key_of[11], 71), 0)
    return {"features": features, "out_grad": out_grad, "reduce_weight": reduce_weight, "spatial_weight": spatial_weight, "expand_weight": expand_weight, "project_weight": project_weight, "reduce_bias": reduce_bias, "spatial_bias": spatial_bias, "output_bias": output_bias, "live_count": live_count, "neighbours": neighbours}


def outer_sum(left, right):
    return lax.dot_general(left, right, (((0,), (0,)), ((), ())), preferred_element_type=jnp.float32)

def times_transposed(left, right):
    return lax.dot_general(left, right, (((1,), (1,)), ((), ())), preferred_element_type=jnp.float32)

def silu_value(value):
    return value * jax.nn.sigmoid(value)

def silu_slope(value):
    sig = jax.nn.sigmoid(value)
    return sig * (1.0 + value * (1.0 - sig))

def pick_rows(table, links):
    valid = links >= 0
    taken = jnp.take(table, jnp.maximum(links, 0).astype(jnp.int32), axis=0)
    shape = (links.shape[0],) + (1,) * (table.ndim - 1)
    return jnp.where(valid.reshape(shape), taken, jnp.zeros_like(taken))

def tile_pass(padded, strided, upstream, alive, spatial_weight, expand_weight, project_weight, spatial_bias, output_bias):
    side = upstream.shape[0]
    patches = jnp.concatenate([padded[row_off:row_off + 2 * side:2, col_off:col_off + 2 * side:2] for row_off in range(3) for col_off in range(3)], -1).reshape(side * side, -1)
    pre_spatial = jnp.dot(patches, spatial_weight, preferred_element_type=jnp.float32) + spatial_bias
    middle = silu_value(pre_spatial).astype(jnp.bfloat16)
    flat_strided = strided.reshape(side * side, -1)
    pre_out = jnp.dot(middle, expand_weight, preferred_element_type=jnp.float32) + jnp.dot(flat_strided, project_weight, preferred_element_type=jnp.float32) + output_bias
    flat_up = upstream.reshape(side * side, -1).astype(jnp.float32)
    gated_out = jnp.where(alive, flat_up * silu_slope(pre_out), jnp.zeros_like(pre_out)).astype(jnp.bfloat16)
    grad_expand = outer_sum(middle, gated_out)
    grad_project = outer_sum(flat_strided, gated_out)
    back_mid = times_transposed(gated_out, expand_weight)
    gated_mid = (back_mid * silu_slope(pre_spatial)).astype(jnp.bfloat16)
    grad_spatial = outer_sum(patches, gated_mid)
    chan_mid = spatial_weight.shape[1]
    back_patch = times_transposed(gated_mid, spatial_weight).reshape(side, side, 9, chan_mid)
    back_padded = jnp.zeros((2 * side + 1, 2 * side + 1, chan_mid), jnp.float32)
    for row_off in range(3):
        for col_off in range(3):
            placed = lax.pad(back_patch[:, :, 3 * row_off + col_off], jnp.zeros((), jnp.float32), [(row_off, 2 - row_off, 1), (col_off, 2 - col_off, 1), (0, 0, 0)])
            back_padded = back_padded + placed
    back_short = times_transposed(gated_out, project_weight).reshape(side, side, -1)
    return (grad_spatial, grad_expand, grad_project, back_padded, back_short)

def reference(features, out_grad, reduce_weight, spatial_weight, expand_weight, project_weight, reduce_bias, spatial_bias, output_bias, live_count, neighbours):
    scale = 1.0 / math.sqrt(SLIDES * TILES * S * S)
    width_in = 2 * S
    total_reduce = jnp.zeros((CIN, CM), jnp.float32)
    total_spatial = jnp.zeros((9 * CM, CM), jnp.float32)
    total_expand = jnp.zeros((CM, COUT), jnp.float32)
    total_project = jnp.zeros((CIN, COUT), jnp.float32)
    results = []
    for slide in range(SLIDES):
        inputs = features[slide]
        links = neighbours[slide]
        slot_ids = jnp.arange(TILES, dtype=jnp.int32)
        live = slot_ids % TILES_DEV < jnp.repeat(live_count[slide], TILES_DEV)
        flat_in = inputs.reshape(-1, CIN)
        pre_reduce = jnp.dot(flat_in, reduce_weight, preferred_element_type=jnp.float32) + reduce_bias
        hidden = silu_value(pre_reduce).astype(jnp.bfloat16).reshape(TILES, width_in, width_in, CM)
        slope_hidden = silu_slope(pre_reduce).reshape(TILES, width_in, width_in, CM)
        last_rows = hidden[:, width_in - 1]
        last_cols = hidden[:, :, width_in - 1]
        above = pick_rows(last_rows, links[:, 1])
        before = pick_rows(last_cols, links[:, 3])
        corner = pick_rows(last_rows, links[:, 0])[:, width_in - 1]
        first_line = jnp.concatenate([corner[:, None], above], 1)
        body_lines = jnp.concatenate([before[:, :, None], hidden], 2)
        padded_all = jnp.concatenate([first_line[:, None], body_lines], 1)
        strided_all = inputs[:, ::2, ::2]

        def scan_step(carry, items):
            padded, strided, upstream, alive = items
            grad_spatial, grad_expand, grad_project, back_padded, back_short = tile_pass(padded, strided, upstream, alive, spatial_weight, expand_weight, project_weight, spatial_bias, output_bias)
            new_carry = (carry[0] + grad_spatial, carry[1] + grad_expand, carry[2] + grad_project)
            return (new_carry, (back_padded, back_short))
        init = (jnp.zeros((9 * CM, CM), jnp.float32), jnp.zeros((CM, COUT), jnp.float32), jnp.zeros((CIN, COUT), jnp.float32))
        sums, stacked = lax.scan(scan_step, init, (padded_all, strided_all, out_grad[slide], live))
        back_padded, back_short = stacked
        top_rims = back_padded[:, 0]
        side_rims = back_padded[:, 1:, 0]
        inner = back_padded[:, 1:, 1:]
        from_below = pick_rows(top_rims, links[:, 6])[:, 1:]
        from_after = pick_rows(side_rims, links[:, 4])
        from_diag = pick_rows(top_rims, links[:, 7])[:, 0]
        back_hidden = inner.at[:, width_in - 1].add(from_below)
        back_hidden = back_hidden.at[:, :, width_in - 1].add(from_after)
        back_hidden = back_hidden.at[:, width_in - 1, width_in - 1].add(from_diag)
        gated_hidden = (back_hidden * slope_hidden).astype(jnp.bfloat16)
        flat_gated = gated_hidden.reshape(-1, CM)
        total_reduce = total_reduce + outer_sum(flat_in, flat_gated)
        total_spatial = total_spatial + sums[0]
        total_expand = total_expand + sums[1]
        total_project = total_project + sums[2]
        back_in = times_transposed(flat_gated, reduce_weight).reshape(TILES, width_in, width_in, CIN)
        back_in = back_in.at[:, ::2, ::2].add(back_short)
        results.append(back_in.astype(jnp.bfloat16))
    feature_grad = jnp.stack(results, 0)
    return (feature_grad, total_reduce * scale, total_spatial * scale, total_expand * scale, total_project * scale)
```

```python
import math

import jax
import jax.numpy as jnp
from jax import lax
from jax.experimental import pallas as pl
from jax.experimental.pallas import tpu as pltpu
from jax.sharding import PartitionSpec as P

F32 = jnp.float32
BF16 = jnp.bfloat16
MESH = pl.DeviceIdType.MESH
SLOTS = 4
SIDE = 32
CHUNK = 16
STEPS = SIDE // CHUNK
PIXELS = CHUNK * SIDE
LINES = 2 * CHUNK

LINE_ROWS = (128, 144, 32, 64)
PLANE_BLOCKS = (8, 9, 0, 4)


def dot(left, right):
    return lax.dot_general(left, right, (((1,), (0,)), ((), ())), preferred_element_type=F32)


def dot_tn(left, right):
    return lax.dot_general(left, right, (((0,), (0,)), ((), ())), preferred_element_type=F32)


def silu_pair(half):
    th = jnp.tanh(half)
    product = half * th
    return half + product, (1.0 + th) + (half - product * th)


def twice_slope(half):
    th = jnp.tanh(half)
    return (1.0 + th) + half * (1.0 - th * th)


def halved(weight):
    return (weight.astype(F32) * 0.5).astype(BF16)


def flip(weight):
    return weight.astype(F32).T.astype(BF16)


def iota(shape, axis):
    return lax.broadcasted_iota(jnp.int32, shape, axis)


def one_hot(flag):
    return jnp.where(flag, 1.0, 0.0).astype(BF16)


def kernel(
    feat_hbm, og_hbm, wr_ref, ws_ref, we_ref, wp_ref, br_ref, bs_ref, bo_ref, live_ref, link_ref,
    feat, exp_out, pro_out, spa_out, red_out,
    og, even, odd, slope_e, slope_o, mx, go_buf, gcat, gh_nat,
    s1, s2a, s2b,
    wrh, wq, wqt_e, wqt_o, wep, wet, wpt, wrt, place, place_b, sel, sel_f, place_g, place_0,
    lhs_b, x_b, og_b, fx_b,
    edge_h, info, info_r, route_r, route_c, route_d,
    msg1, mid1, fan1, got1, halo,
    msg2, mid2, fan2, got2,
    acc_ep, acc_e, acc_o, acc_r,
    ar0, ar1, ar2, ar3, rs0, rs1, rs2, rs3, sh0, sh1, sh2, sh3, pr0, pr1, pr2, pr3, fb,
    fin0, fin1, fin2, fin3, ag0, ag1, ag2, ag3,
    feat_sem, og_sem,
    info_s, info_q, a1_s, a1_q, b1_s, b1_q, a2_s, a2_q, b2_s, b2_q,
    l1_s, l1_q, p1_s, p1_q, p2_s, p2_q, l2_s, l2_q,
):
    dp = lax.axis_index("dp")
    space = lax.axis_index("space")
    core = dp % 2
    z_hi = dp // 2
    z_lo = space % 2
    cy = (space // 2) % 4
    cx = space // 8
    cz = z_hi * 2 + z_lo

    def device(x, y, z, c):
        return ((z // 2) * 2 + c, (x * 4 + y) * 2 + z % 2)

    def x_peer(d):
        return (dp, (((cx + d) % 4) * 4 + cy) * 2 + z_lo)

    my_fan = cy * 2 + z_lo

    def fan_index(d):
        return (my_fan + d) % 8

    def fan_peer(d):
        return (dp, cx * 8 + fan_index(d))

    line_me = (cx * 2 + core, cy * 2 + core, cz * 2 + core, cz * 2 + core)
    plane_me = (cy * 4 + cz, cx * 4 + cz, cx * 4 + cy, cx * 4 + cy)

    def line_device(which, index):
        pos, c = index // 2, index % 2
        if which == 0:
            return device(pos, cy, cz, c)
        if which == 1:
            return device(cx, pos, cz, c)
        return device(cx, cy, pos, c)

    def plane_device(which, index):
        a, b = index // 4, index % 4
        if which == 0:
            return device(cx, a, b, core)
        if which == 1:
            return device(a, cy, b, core)
        return device(a, b, cz, core)

    feat_in = [pltpu.make_async_copy(feat_hbm.at[0, t], feat.at[t], feat_sem.at[t]) for t in range(SLOTS)]
    og_in = [pltpu.make_async_copy(og_hbm.at[0, t], og.at[t], og_sem.at[t]) for t in range(SLOTS)]
    for copy in feat_in + og_in:
        copy.start()

    barrier = pltpu.get_barrier_semaphore()
    peers = []
    for dx in range(4):
        for dy in range(4):
            for dz in range(4):
                moved = (dx > 0) + (dy > 0) + (dz > 0)
                for dc in range(2):
                    if (moved <= 1 and moved + dc > 0) or (moved == 2 and dc == 0):
                        peers.append((dx, dy, dz, dc))
    for dx, dy, dz, dc in peers:
        pl.semaphore_signal(
            barrier, inc=1, device_id=device((cx + dx) % 4, (cy + dy) % 4, (cz + dz) % 4, (core + dc) % 2),
            device_id_type=MESH,
        )

    wrh[...] = halved(wr_ref[...])
    zero = jnp.zeros((128, 128), BF16)

    def tap(r, c):
        return halved(ws_ref[(3 * r + c) * 128 : (3 * r + c + 1) * 128, :])

    blocks = (
        (tap(1, 1), zero), (tap(1, 2), tap(1, 0)), (tap(2, 1), zero),
        (tap(2, 2), tap(2, 0)), (tap(0, 1), zero), (tap(0, 2), tap(0, 0)),
    )
    for row, (first, second) in enumerate(blocks):
        wq[row * 128 : (row + 1) * 128, 0:128] = first
        wq[row * 128 : (row + 1) * 128, 128:256] = second
    sel_f[...] = one_hot(iota((64, 1024), 1) == iota((64, 1024), 0) * 16 + 15)
    lane = iota((1, 128), 1)
    for way in range(8):
        row = jnp.full((1, 128), link_ref[0, 0, way].astype(F32), F32)
        for t in range(1, SLOTS):
            row = jnp.where(lane >= t * 32, link_ref[0, t, way].astype(F32), row)
        info[way : way + 1, :] = row
    wqt_e[...] = flip(wq[0:256, :])
    wqt_o[0:256, :] = flip(wq[256:512, :])
    wqt_o[256:512, :] = flip(wq[512:768, :])
    wep[0:128, :] = halved(we_ref[...])
    wep[128:384, :] = halved(wp_ref[...])
    wet[...] = flip(halved(we_ref[...]))
    wpt[...] = flip(wp_ref[...])
    wrt[...] = flip(wr_ref[...])

    px, col = iota((1024, 128), 0), iota((1024, 128), 1)
    pi, pj = px >> 5, px & 31
    place[...] = one_hot(
        ((col < 32) & (pi == 0) & (pj == col))
        | ((col >= 32) & (col < 64) & (pj == 0) & (pi == col - 32))
        | ((col == 64) & (px == 0))
    )
    m, k = iota((256, 128), 0) & 63, iota((256, 128), 1)
    place_b[...] = one_hot(
        ((m < 32) & (k == m)) | ((m == 0) & ((k == 32) | (k == 64)))
        | ((m >= 32) & (k == m)) | ((m == 32) & ((k == 0) | (k == 64)))
    )
    sel[...] = one_hot(iota((32, 512), 1) == iota((32, 512), 0) * 16)
    place_g[...] = one_hot(iota((512, 32), 0) == iota((512, 32), 1) * 16 + 15)
    place_0[...] = one_hot(iota((512, 32), 0) == iota((512, 32), 1) * 16)

    odd[:, 0, :, :] = jnp.zeros((SLOTS, SIDE, 256), BF16)
    gcat[:, SIDE, :, :] = jnp.zeros((SLOTS, SIDE, 256), BF16)
    s2a[...] = jnp.zeros_like(s2a)
    s2b[...] = jnp.zeros_like(s2b)
    halo[...] = jnp.zeros_like(halo)
    for acc in (acc_ep, acc_e, acc_o, acc_r):
        acc[...] = jnp.zeros_like(acc)

    for t in range(SLOTS):
        feat_in[t].wait()
        fx_b[t * 128 : t * 128 + 64, :] = feat[t, 63]
        strip = feat[t, :, 48:64, :].reshape(1024, 256)
        fx_b[t * 128 + 64 : t * 128 + 128, :] = dot(sel_f[...], strip).astype(BF16)
    s1[0:512, :] = silu_pair(dot(fx_b[...], wrh[...]) + 0.5 * br_ref[...])[0]

    def every_other(offset):
        return jnp.concatenate(
            [s1[pl.ds(t * 128 + offset, 32, stride=2), :] for t in range(SLOTS)], 0
        ).astype(BF16)

    oe_row, oo_row, eo_col, oo_col = every_other(0), every_other(1), every_other(64), every_other(65)
    for at, rows in enumerate((oe_row, oo_row, eo_col, oo_col)):
        edge_h[at] = rows
    inner_at = iota((128, 128), 0) & 31
    q_row = dot(jnp.concatenate([oe_row, oo_row], 1), wq[512:768, :])
    below = q_row[:, 0:128] + jnp.where(inner_at >= 1, pltpu.roll(q_row[:, 128:256], 1, 0), 0.0)
    right = dot(jnp.concatenate([eo_col, oo_col], 1),
                jnp.concatenate([wq[128:256, 128:256], wq[384:512, 128:256]], 0))
    right_up = dot(oo_col, wq[640:768, 128:256])
    right = right + jnp.where(inner_at >= 1, pltpu.roll(right_up, 1, 0), 0.0)
    s1[0:128, :] = q_row[:, 128:256]
    first_row = iota((16, 128), 0) == 0
    for t in range(SLOTS):
        msg1[t, 0:32, :] = below[t * 32 : (t + 1) * 32].astype(BF16)
        msg1[t, 32:64, :] = right[t * 32 : (t + 1) * 32].astype(BF16)
        corner = jnp.broadcast_to(s1[t * 32 + 31 : t * 32 + 32, :], (16, 128))
        msg1[t, 64:80, :] = jnp.where(first_row, corner, 0.0).astype(BF16)

    def gather_start(msg, mid, send, recv):
        copies = []
        for d in range(1, 4):
            copy = pltpu.make_async_remote_copy(
                msg, mid.at[d], send.at[d], recv.at[d], device_id=x_peer(d), device_id_type=MESH
            )
            copy.start()
            copies.append(copy)
        mid[0] = msg[...]
        return copies

    def fan_out(copies, mid, fan, got, ways, corner_at, send, recv):
        for copy in copies:
            copy.wait()
        lead = max(corner_at - 16, 0)
        rows_block = mid[:, :, 0:32, :].reshape(512, 128)
        cols_block = mid[:, :, 32:64, :].reshape(512, 128)
        corner_block = mid[:, :, lead : lead + 32, :].reshape(512, 128)
        goals = [
            jnp.concatenate([info_r[source, way : way + 1, :] for source in range(4)], 1) for way in ways
        ]
        row, column = iota((128, 512), 0), iota((128, 512), 1)
        for route, goal in ((route_r, goals[0]), (route_c, goals[1])):
            route[...] = jnp.where((row & 31) == (column & 31), goal - (row >> 5).astype(F32), -9.0)
        row, column = iota((16, 512), 0), iota((16, 512), 1)
        route_d[...] = jnp.where(
            (row < SLOTS) & ((column & 31) == corner_at - lead), goals[2] - row.astype(F32), -9.0
        )
        for p in range(8):
            base = ((cx * 8 + p) * SLOTS).astype(F32)
            for route, block, at in ((route_r, rows_block, 0), (route_c, cols_block, 32)):
                picked = dot(one_hot(route[...] == base), block).astype(BF16)
                for slot in range(SLOTS):
                    fan[p, slot * 64 + at : slot * 64 + at + 32, :] = picked[slot * 32 : slot * 32 + 32]
            fan[p, 256:272, :] = dot(one_hot(route_d[...] == base), corner_block).astype(BF16)
        sends = []
        for d in range(1, 8):
            copy = pltpu.make_async_remote_copy(
                fan.at[fan_index(d)], got.at[d], send.at[d], recv.at[d],
                device_id=fan_peer(d), device_id_type=MESH,
            )
            copy.start()
            sends.append(copy)
        got[0] = fan[my_fan]
        return sends

    def collect(got):
        total = got[0]
        for d in range(1, 8):
            total = total + got[d]
        return total

    pl.semaphore_wait(barrier, len(peers))

    info_copies = []
    for d in range(1, 4):
        copy = pltpu.make_async_remote_copy(
            info, info_r.at[d], info_s.at[d], info_q.at[d], device_id=x_peer(d), device_id_type=MESH
        )
        copy.start()
        info_copies.append(copy)
    gather1 = gather_start(msg1, mid1, a1_s, a1_q)
    info_r[0] = info[...]

    def reduce_step(step, _):
        t, c = step // STEPS, step % STEPS
        row0 = pl.multiple_of(c * LINES, 16)
        x = feat[t, pl.ds(row0, LINES)].reshape(4 * PIXELS, 256)
        s1[...] = dot(x, wrh[...]) + 0.5 * br_ref[...]
        for i in range(CHUNK):
            at = c * CHUNK + i
            for r, (plane, slope, shift) in enumerate(((even, slope_e, 0), (odd, slope_o, 1))):
                for e in range(2):
                    act, slp = silu_pair(s1[pl.ds(i * 128 + r * 64 + e, 32, stride=2), :])
                    plane[t, at + shift, :, e * 128 : (e + 1) * 128] = act.astype(BF16)
                    slope[t, at, :, e * 128 : (e + 1) * 128] = slp.astype(BF16)
            line = feat[t, row0 + 2 * i].astype(F32)
            s2a[i * 64 : (i + 1) * 64, :] = line[:, 0:128]
            s2b[i * 64 : (i + 1) * 64, :] = line[:, 128:256]
            mx[t, at, :, 128:256] = s2a[pl.ds(i * 64, 32, stride=2), :].astype(BF16)
            mx[t, at, :, 256:384] = s2b[pl.ds(i * 64, 32, stride=2), :].astype(BF16)
        return 0

    half = SLOTS * STEPS // 2
    lax.fori_loop(0, half, reduce_step, 0)
    for copy in info_copies:
        copy.wait()
    sends1 = fan_out(gather1, mid1, fan1, got1, (6, 4, 7), 64, b1_s, b1_q)
    lax.fori_loop(half, 2 * half, reduce_step, 0)
    s2a[...] = jnp.zeros_like(s2a)
    s2b[...] = jnp.zeros_like(s2b)
    def middle_part(lhs, halo_sum, follows, x, grad, alive):
        q = dot(lhs, wq[...])
        pre = q[:, 0:128] + jnp.where(follows, pltpu.roll(q[:, 128:256], 1, 0), 0.0) + halo_sum + 0.5 * bs_ref[...]
        mid, slope_mid = silu_pair(pre)
        mid = mid.astype(BF16)
        pre_out = dot(jnp.concatenate([mid, x], 1), wep[...]) + 0.5 * bo_ref[...]
        gated = (grad.astype(F32) * alive * twice_slope(pre_out)).astype(BF16)
        return mid, gated, dot(gated, wet[...]) * slope_mid

    at_row = iota((PIXELS, 128), 0) & 31
    follows = at_row >= 1
    leads = at_row < 31

    for copy in og_in:
        copy.wait()
    count = live_ref[0, 0]

    def middle_step(with_halo, step):
        t, c = step // STEPS, step % STEPS
        i0 = c * CHUNK
        lhs = jnp.concatenate(
            [
                even[t, pl.ds(i0, CHUNK)].reshape(PIXELS, 256),
                odd[t, pl.ds(i0 + 1, CHUNK)].reshape(PIXELS, 256),
                odd[t, pl.ds(i0, CHUNK)].reshape(PIXELS, 256),
            ],
            1,
        )
        halo_sum = 0.0
        if with_halo:
            halo_sum = dot(place[pl.ds(pl.multiple_of(c * PIXELS, 256), PIXELS), :], halo[t])
        x = mx[t, pl.ds(i0, CHUNK), :, 128:384].reshape(PIXELS, 256)
        grad = og[t, pl.ds(i0, CHUNK)].reshape(PIXELS, 512)
        alive = jnp.where(t < count, 0.5, 0.0)
        mid, gated, g = middle_part(lhs, halo_sum, follows, x, grad, alive)
        mx[t, pl.ds(i0, CHUNK), :, 0:128] = mid.reshape(CHUNK, SIDE, 128)
        go_buf[t, pl.ds(i0, CHUNK)] = gated.reshape(CHUNK, SIDE, 512)
        ahead = jnp.where(leads, pltpu.roll(g, PIXELS - 1, 0), 0.0)
        gcat[t, pl.ds(i0, CHUNK), :, 0:128] = g.astype(BF16).reshape(CHUNK, SIDE, 128)
        gcat[t, pl.ds(i0, CHUNK), :, 128:256] = ahead.astype(BF16).reshape(CHUNK, SIDE, 128)

    def middle_loop(with_halo, first, last):
        def step(at, _):
            middle_step(with_halo, at)
            return 0

        lax.fori_loop(first * STEPS, last * STEPS, step, 0)

    def outer_tile(t, _):
        acc_ep[...] += dot_tn(mx[t].reshape(1024, 384), go_buf[t].reshape(1024, 512))
        return 0

    middle_loop(False, 0, 2)

    for copy in sends1:
        copy.wait()
    sums1 = collect(got1)
    corners1 = sums1[256:272].astype(F32)
    for t in range(SLOTS):
        halo[t, 0:64, :] = sums1[t * 64 : t * 64 + 64]
        corner = jnp.broadcast_to(corners1[t : t + 1], (16, 128))
        halo[t, 64:80, :] = jnp.where(first_row, corner, 0.0).astype(BF16)

    for t in range(SLOTS):
        lo, hi = t * 64, t * 64 + 32
        lhs_b[lo:hi, 0:256] = even[t, 0]
        lhs_b[lo:hi, 256:512] = odd[t, 1]
        lhs_b[lo:hi, 512:768] = odd[t, 0]
        x_b[lo:hi, :] = mx[t, 0, :, 128:384]
        og_b[lo:hi, :] = og[t, 0]
        lo, hi = hi, hi + 32
        pick = sel[...]
        lhs_b[lo:hi, 0:256] = dot(pick, even[t, :, 0:16, :].reshape(512, 256)).astype(BF16)
        lhs_b[lo:hi, 256:512] = dot(pick, odd[t, 1:33, 0:16, :].reshape(512, 256)).astype(BF16)
        lhs_b[lo:hi, 512:768] = dot(pick, odd[t, 0:32, 0:16, :].reshape(512, 256)).astype(BF16)
        x_b[lo:hi, :] = dot(pick, mx[t, :, 0:16, 128:384].reshape(512, 256)).astype(BF16)
        og_b[lo:hi, :] = dot(pick, og[t, :, 0:16, :].reshape(512, 512)).astype(BF16)

    spot = iota((256, 128), 0)
    halo_b = jnp.concatenate(
        [dot(place_b[t * 64 : (t + 1) * 64, :], halo[t]) for t in range(SLOTS)], 0
    )
    alive_b = jnp.where(iota((256, 1), 0) >> 6 < count, 0.5, 0.0)
    edge = ((spot & 63) >= 1) & ((spot & 63) < 32)
    mid_edge, gated_edge, g_edge = middle_part(lhs_b[...], halo_b, edge, x_b[...], og_b[...], alive_b)
    for t in range(SLOTS):
        msg2[t] = g_edge[t * 64 : (t + 1) * 64].astype(BF16)
    gather2 = gather_start(msg2, mid2, a2_s, a2_q)

    def put_column(ref, t, lanes, column):
        width = lanes.stop - lanes.start
        placed = dot(place_0[...], column)
        old = ref[t, 0:32, 0:16, lanes].reshape(512, width).astype(F32)
        first = (iota((512, width), 0) & 15) == 0
        ref[t, 0:32, 0:16, lanes] = jnp.where(first, placed, old).astype(BF16).reshape(32, 16, width)

    for t in range(2):
        lo, hi = t * 64, t * 64 + 32
        put_column(mx, t, slice(0, 128), mid_edge[hi : hi + 32])
        put_column(go_buf, t, slice(0, 512), gated_edge[hi : hi + 32])
        put_column(gcat, t, slice(0, 128), g_edge[hi : hi + 32].astype(BF16))
        mx[t, 0, :, 0:128] = mid_edge[lo:hi]
        go_buf[t, 0] = gated_edge[lo:hi]
        row = g_edge[lo:hi]
        gcat[t, 0, :, 0:128] = row.astype(BF16)
        gcat[t, 0, :, 128:256] = jnp.where(iota((32, 128), 0) < 31, pltpu.roll(row, 31, 0), 0.0).astype(BF16)

    middle_loop(True, 2, 3)
    lax.fori_loop(0, 1, outer_tile, 0)
    sends2 = fan_out(gather2, mid2, fan2, got2, (1, 3, 0), 0, b2_s, b2_q)
    middle_loop(True, 3, 4)
    lax.fori_loop(1, SLOTS, outer_tile, 0)

    ar, rs, sh, pr = (ar0, ar1, ar2, ar3), (rs0, rs1, rs2, rs3), (sh0, sh1, sh2, sh3), (pr0, pr1, pr2, pr3)
    fin, ag = (fin0, fin1, fin2, fin3), (ag0, ag1, ag2, ag3)

    def line_scatter(which):
        rows = LINE_ROWS[which]
        copies = []
        for d in range(1, 8):
            target = (line_me[which] + d) % 8
            copy = pltpu.make_async_remote_copy(
                ar[which].at[pl.ds(pl.multiple_of(target * rows, 16), rows)], rs[which].at[d],
                l1_s.at[which, d], l1_q.at[which, d],
                device_id=line_device(which, target), device_id_type=MESH,
            )
            copy.start()
            copies.append(copy)
        return copies

    def plane_copy(which, d):
        target = (plane_me[which] + d) % 16
        return target, pltpu.make_async_remote_copy(
            sh[which].at[pl.ds(pl.multiple_of(target * 16, 16), 16)], pr[which].at[d],
            p1_s.at[which, d], p1_q.at[which, d],
            device_id=plane_device(which, target), device_id_type=MESH,
        )

    def plane_whole_copy(which, d):
        return pltpu.make_async_remote_copy(
            sh[which], pr[which].at[d], p1_s.at[which, d], p1_q.at[which, d],
            device_id=plane_device(which, (plane_me[which] + d) % 16), device_id_type=MESH,
        )

    def plane_scatter(which, copies):
        rows = LINE_ROWS[which]
        for copy in copies:
            copy.wait()
        total = ar[which][pl.ds(pl.multiple_of(line_me[which] * rows, 16), rows), :].astype(F32)
        for d in range(1, 8):
            total = total + rs[which][d].astype(F32)
        sh[which][...] = total.astype(BF16)
        if PLANE_BLOCKS[which] == 0:
            for d in range(1, 16):
                plane_whole_copy(which, d).start()
            return
        for d in range(1, 16):
            target, copy = plane_copy(which, d)

            @pl.when(target < PLANE_BLOCKS[which])
            def _(copy=copy):
                copy.start()

    def plane_spread_copy(which, d):
        me = pl.multiple_of(plane_me[which] * 16, 16)
        return pltpu.make_async_remote_copy(
            fb.at[which], fin[which].at[pl.ds(me, 16)],
            p2_s.at[which, d], p2_q.at[which, d],
            device_id=plane_device(which, (plane_me[which] + d) % 16), device_id_type=MESH,
        )

    def plane_spread(which):
        me = plane_me[which]

        @pl.when(me < PLANE_BLOCKS[which])
        def _():
            for d in range(1, 16):
                pltpu.make_async_remote_copy(
                    fb.at[which], pr[which].at[d], p1_s.at[which, d], p1_q.at[which, d],
                    device_id=plane_device(which, (me + d) % 16), device_id_type=MESH,
                ).wait_recv()
            at = pl.ds(pl.multiple_of(me * 16, 16), 16)
            total = sh[which][at, :].astype(F32)
            for d in range(1, 16):
                total = total + pr[which][d].astype(F32)
            fb[which] = total.astype(BF16)
            for d in range(1, 16):
                plane_spread_copy(which, d).start()
            fin[which][at, :] = total.astype(BF16)

    def line_spread(which):
        me = plane_me[which]
        if PLANE_BLOCKS[which] == 0:
            total = sh[which][...].astype(F32)
            for d in range(1, 16):
                plane_whole_copy(which, d).wait()
                total = total + pr[which][d].astype(F32)
            fin[which][...] = total.astype(BF16)
        for d in range(1, 16):
            if PLANE_BLOCKS[which] == 0:
                break
            source = (me + 16 - d) % 16

            @pl.when(source < PLANE_BLOCKS[which])
            def _(d=d, source=source):
                at = pl.ds(pl.multiple_of(source * 16, 16), 16)
                pltpu.make_async_remote_copy(
                    fb.at[which], fin[which].at[at], p2_s.at[which, d], p2_q.at[which, d],
                    device_id=plane_device(which, (me + d) % 16), device_id_type=MESH,
                ).wait_recv()

        copies = []
        for d in range(1, 8):
            copy = pltpu.make_async_remote_copy(
                fin[which], ag[which].at[line_me[which]],
                l2_s.at[which, d], l2_q.at[which, d],
                device_id=line_device(which, (line_me[which] + d) % 8), device_id_type=MESH,
            )
            copy.start()
            copies.append(copy)
        ag[which][line_me[which]] = fin[which][...]
        return copies

    def line_finish(which, copies):
        rows = LINE_ROWS[which]
        for d in range(1, 8):
            source = (line_me[which] + 8 - d) % 8
            copies[d - 1].wait_send()
            pltpu.make_async_remote_copy(
                fin[which], ag[which].at[source], l2_s.at[which, d], l2_q.at[which, d],
                device_id=line_device(which, (line_me[which] + d) % 8), device_id_type=MESH,
            ).wait_recv()
        if PLANE_BLOCKS[which] > 0:
            for d in range(1, 16):
                target, copy = plane_copy(which, d)

                @pl.when(target < PLANE_BLOCKS[which])
                def _(copy=copy):
                    copy.wait_send()

            @pl.when(plane_me[which] < PLANE_BLOCKS[which])
            def _():
                for d in range(1, 16):
                    plane_spread_copy(which, d).wait_send()

        return ag[which][...].reshape(8 * rows, 128)

    for block in range(4):
        ar0[block * 256 : (block + 1) * 256, :] = acc_ep[128:384, block * 128 : (block + 1) * 128].astype(BF16)
        ar3[block * 128 : (block + 1) * 128, :] = acc_ep[0:128, block * 128 : (block + 1) * 128].astype(BF16)
    line0, line3 = line_scatter(0), line_scatter(3)

    def spatial_tile(t, _):
        g0 = gcat[t, 0:32].reshape(1024, 256)
        g1 = gcat[t, 1:33].reshape(1024, 256)
        acc_e[...] += dot_tn(even[t].reshape(1024, 256), g0)
        acc_o[...] += dot_tn(odd[t, 1:33].reshape(1024, 256), jnp.concatenate([g0, g1], 1))
        return 0

    lax.fori_loop(0, SLOTS, spatial_tile, 0)

    for copy in sends2:
        copy.wait()
    last_at = iota((32, 128), 0) == 31
    under, under_next, beside, beside_next = [], [], [], []
    plane_scatter(0, line0)
    plane_scatter(3, line3)
    sums2 = collect(got2).astype(F32)
    for t in range(SLOTS):
        rims = sums2[t * 64 : t * 64 + 64]
        diag = jnp.broadcast_to(sums2[256 + t : 257 + t], (32, 128))
        under.append(rims[0:32].astype(BF16))
        under_next.append(jnp.where(last_at, diag, pltpu.roll(rims[0:32], 31, 0)).astype(BF16))
        beside.append(rims[32:64].astype(BF16))
        beside_next.append(jnp.where(last_at, 0.0, pltpu.roll(rims[32:64], 31, 0)).astype(BF16))
        gcat[t, 32, :, 0:128] = under[t]
        gcat[t, 32, :, 128:256] = under_next[t]
        placed = dot(place_g[...], beside[t])
        strip = gcat[t, 0:32, 16:32, 128:256].reshape(512, 128).astype(F32) + placed
        gcat[t, 0:32, 16:32, 128:256] = strip.astype(BF16).reshape(32, 16, 128)
    under, under_next = jnp.concatenate(under, 0), jnp.concatenate(under_next, 0)
    beside, beside_next = jnp.concatenate(beside, 0), jnp.concatenate(beside_next, 0)
    acc_e[128:256, 128:256] += dot_tn(edge_h[2], beside)
    acc_o[128:256, 128:256] += dot_tn(edge_h[3], beside)
    acc_o[0:128, 256:384] += dot_tn(edge_h[0], under)
    acc_o[128:256, 256:384] += dot_tn(edge_h[1], under)
    acc_o[128:256, 384:512] += dot_tn(edge_h[1], under_next) + dot_tn(edge_h[3], beside_next)

    def back_step(step, _):
        t, c = step // STEPS, step % STEPS
        i0 = c * CHUNK
        g0 = gcat[t, pl.ds(i0, CHUNK)].reshape(PIXELS, 256)
        g1 = gcat[t, pl.ds(i0 + 1, CHUNK)].reshape(PIXELS, 256)
        back_e = dot(g0, wqt_e[...])
        back_o = dot(jnp.concatenate([g0, g1], 1), wqt_o[...])
        gh_e = back_e * slope_e[t, pl.ds(i0, CHUNK)].reshape(PIXELS, 256).astype(F32)
        gh_o = back_o * slope_o[t, pl.ds(i0, CHUNK)].reshape(PIXELS, 256).astype(F32)
        for i in range(CHUNK):
            for r, gh in enumerate((gh_e, gh_o)):
                for e in range(2):
                    s1[pl.ds(i * 128 + r * 64 + e, 32, stride=2), :] = gh[
                        i * 32 : (i + 1) * 32, e * 128 : (e + 1) * 128
                    ]
        row0 = pl.multiple_of(c * LINES, 16)
        natural = s1[...].astype(BF16)
        gh_nat[t, pl.ds(row0, LINES)] = natural.reshape(LINES, 64, 128)
        acc_r[...] += dot_tn(natural, feat[t, pl.ds(row0, LINES)].reshape(4 * PIXELS, 256))
        return 0

    for which_tap, block in (
        ((1, 1), acc_e[0:128, 0:128]), ((1, 2), acc_e[128:256, 0:128]), ((1, 0), acc_e[128:256, 128:256]),
        ((2, 1), acc_o[0:128, 0:128]), ((2, 2), acc_o[128:256, 0:128]), ((2, 0), acc_o[128:256, 128:256]),
        ((0, 1), acc_o[0:128, 256:384]), ((0, 2), acc_o[128:256, 256:384]), ((0, 0), acc_o[128:256, 384:512]),
    ):
        at = (3 * which_tap[0] + which_tap[1]) * 128
        ar1[at : at + 128, :] = block.astype(BF16)
    line1 = line_scatter(1)
    lax.fori_loop(0, 2 * STEPS, back_step, 0)
    plane_spread(0)
    plane_spread(3)
    lax.fori_loop(2 * STEPS, 3 * STEPS, back_step, 0)
    plane_scatter(1, line1)
    lax.fori_loop(3 * STEPS, 4 * STEPS, back_step, 0)
    ar2[...] = acc_r[...].T.astype(BF16)
    line2 = line_scatter(2)
    spread0 = line_spread(0)
    spread3 = line_spread(3)

    def feature_step(step, _):
        t, c = step // STEPS, step % STEPS
        i0 = c * CHUNK
        row0 = pl.multiple_of(c * LINES, 16)
        wide = dot(gh_nat[t, pl.ds(row0, LINES)].reshape(4 * PIXELS, 128), wrt[...])
        short = dot(go_buf[t, pl.ds(i0, CHUNK)].reshape(PIXELS, 512), wpt[...])
        for i in range(CHUNK):
            s2a[pl.ds(i * 64, 32, stride=2), :] = short[i * 32 : (i + 1) * 32, 0:128]
            s2b[pl.ds(i * 64, 32, stride=2), :] = short[i * 32 : (i + 1) * 32, 128:256]
            first = wide[i * 128 : i * 128 + 64]
            feat[t, row0 + 2 * i, :, 0:128] = (first[:, 0:128] + s2a[i * 64 : (i + 1) * 64, :]).astype(BF16)
            feat[t, row0 + 2 * i, :, 128:256] = (first[:, 128:256] + s2b[i * 64 : (i + 1) * 64, :]).astype(BF16)
            feat[t, row0 + 2 * i + 1] = wide[i * 128 + 64 : i * 128 + 128].astype(BF16)
        return 0

    lax.fori_loop(0, 2 * STEPS, feature_step, 0)
    plane_spread(1)
    plane_scatter(2, line2)
    lax.fori_loop(2 * STEPS, 4 * STEPS, feature_step, 0)
    spread1 = line_spread(1)
    spread2 = line_spread(2)
    pro_out[...] = line_finish(0, spread0)
    exp_out[...] = line_finish(3, spread3)
    spa_out[...] = line_finish(1, spread1)
    red_out[...] = line_finish(2, spread2)


def finish_kernel(
    scale, grad_ref, exp_ref, pro_ref, spa_ref, red_ref, out_hbm, red_out, spa_out, exp_out, pro_out, sems
):
    writes = [
        pltpu.make_async_copy(grad_ref.at[t, pl.ds(c * 16, 16)], out_hbm.at[0, t, pl.ds(c * 16, 16)], sems.at[t, c])
        for t in range(SLOTS)
        for c in range(4)
    ]
    for copy in writes:
        copy.start()
    for block in range(4):
        lanes = slice(block * 128, (block + 1) * 128)
        exp_out[:, lanes] = exp_ref[block * 128 : (block + 1) * 128, :].astype(F32) * scale
        pro_out[:, lanes] = pro_ref[block * 256 : (block + 1) * 256, :].astype(F32) * scale
    spa_out[...] = spa_ref[...].astype(F32) * scale
    red_out[...] = red_ref[...].astype(F32) * scale
    for copy in writes:
        copy.wait()


def local(
    features, out_grad, reduce_weight, spatial_weight, expand_weight, project_weight,
    reduce_bias, spatial_bias, output_bias, live_count, neighbours,
):
    scale = 1.0 / math.sqrt(lax.axis_size("dp") * lax.axis_size("space") * SLOTS * SIDE * SIDE)
    vmem = pl.BlockSpec(memory_space=pltpu.VMEM)
    smem = pl.BlockSpec(memory_space=pltpu.SMEM)
    hbm = pl.BlockSpec(memory_space=pl.ANY)
    dma = pltpu.SemaphoreType.DMA

    def buf(shape, dtype=BF16):
        return pltpu.VMEM(shape, dtype)

    scratch = [
        buf((4, 32, 32, 512)), buf((4, 32, 32, 256)), buf((4, 33, 32, 256)),
        buf((4, 32, 32, 256)), buf((4, 32, 32, 256)), buf((4, 32, 32, 384)), buf((4, 32, 32, 512)),
        buf((4, 33, 32, 256)), buf((4, 64, 64, 128)),
        buf((4 * PIXELS, 128), F32), buf((2 * PIXELS, 128), F32), buf((2 * PIXELS, 128), F32),
        buf((256, 128)), buf((768, 256)), buf((256, 256)), buf((512, 256)), buf((384, 512)), buf((512, 128)),
        buf((512, 256)), buf((128, 256)), buf((1024, 128)), buf((256, 128)), buf((32, 512)),
        buf((64, 1024)), buf((512, 32)), buf((512, 32)),
        buf((256, 768)), buf((256, 256)), buf((256, 512)), buf((512, 256)),
        buf((4, 128, 128)), buf((8, 128), F32), buf((4, 8, 128), F32),
        buf((128, 512), F32), buf((128, 512), F32), buf((16, 512), F32),
        buf((4, 80, 128)), buf((4, 4, 80, 128)), buf((8, 272, 128)), buf((8, 272, 128)), buf((4, 128, 128)),
        buf((4, 64, 128)), buf((4, 4, 64, 128)), buf((8, 272, 128)), buf((8, 272, 128)),
        buf((384, 512), F32), buf((256, 256), F32), buf((256, 512), F32), buf((128, 256), F32),
    ]
    scratch += [buf((8 * rows, 128)) for rows in LINE_ROWS]
    scratch += [buf((8, rows, 128)) for rows in LINE_ROWS]
    scratch += [buf((rows, 128)) for rows in LINE_ROWS]
    scratch += [buf((16, 16, 128)), buf((16, 16, 128)), buf((16, 32, 128)), buf((16, 16, 128))]
    scratch += [buf((4, 16, 128))]
    scratch += [buf((rows, 128)) for rows in LINE_ROWS]
    scratch += [buf((8, rows, 128)) for rows in LINE_ROWS]
    scratch += [dma((4,)), dma((4,))]
    scratch += [dma((4,)), dma((4,))]
    scratch += [dma((4,)), dma((4,)), dma((8,)), dma((8,))] * 2
    scratch += [dma((4, 8)), dma((4, 8)), dma((4, 16)), dma((4, 16))]
    scratch += [dma((4, 16)), dma((4, 16)), dma((4, 8)), dma((4, 8))]

    raw = pl.pallas_call(
        kernel,
        out_shape=(
            pltpu.VMEM((4, 64, 64, 256), BF16),
            pltpu.VMEM((512, 128), BF16),
            pltpu.VMEM((1024, 128), BF16),
            pltpu.VMEM((1152, 128), BF16),
            pltpu.VMEM((256, 128), BF16),
        ),
        in_specs=[hbm, hbm] + [vmem] * 7 + [smem, smem],
        out_specs=(vmem, vmem, vmem, vmem, vmem),
        scratch_shapes=scratch,
        compiler_params=pltpu.CompilerParams(
            collective_id=0, has_side_effects=True, vmem_limit_bytes=50 * 1024 * 1024
        ),
        cost_estimate=pl.CostEstimate(flops=24 * 10**9, bytes_accessed=22 * 10**6, transcendentals=5 * 10**6),
    )(
        features, out_grad, reduce_weight, spatial_weight, expand_weight, project_weight,
        reduce_bias.reshape(1, 128), spatial_bias.reshape(1, 128), output_bias.reshape(1, 512),
        live_count, neighbours,
    )

    def finish_body(*refs):
        finish_kernel(scale, *refs)

    return pl.pallas_call(
        finish_body,
        out_shape=(
            jax.ShapeDtypeStruct(features.shape, BF16),
            jax.ShapeDtypeStruct((256, 128), F32),
            jax.ShapeDtypeStruct((1152, 128), F32),
            jax.ShapeDtypeStruct((128, 512), F32),
            jax.ShapeDtypeStruct((256, 512), F32),
        ),
        in_specs=[hbm, vmem, vmem, vmem, vmem],
        out_specs=(hbm, vmem, vmem, vmem, vmem),
        scratch_shapes=[dma((4, 4))],
        compiler_params=pltpu.CompilerParams(vmem_limit_bytes=8 * 1024 * 1024),
    )(*raw)


def solution(mesh):
    wide = P("dp", "space", None, None, None)
    in_specs = (wide, wide, P(), P(), P(), P(), P(), P(), P(), P("dp", "space"), P("dp", "space", None))
    out_specs = (wide, P(), P(), P(), P())
    return jax.shard_map(local, mesh=mesh, in_specs=in_specs, out_specs=out_specs, check_vma=False)
```
